32 devices in a mesh: dp: 8 (over z, x), tensor: 4 (over y, core).
Axes of the slice: x: 2, y: 2, z: 4, core: 2. Of those that a mesh axis runs over, the one named last changes fastest.
Arguments:
- tokens: bfloat16 [8192, 1024], P(('dp', 'tensor')), may hold values from -6 to 6
- memory: bfloat16 [8192, 1024], P(('dp', 'tensor')), may hold values from -6 to 6
- cotangent: bfloat16 [8192, 1024], P(('dp', 'tensor')), may hold values from -6 to 6
- segments: int32 [8, 1024], P('dp'), may hold values from 0 to 3, never falling along the last dimension, each value on 1 to 512 neighbouring positions
- offsets: int32 [8, 4], P('dp'), may hold values from 0 to 1023, as said below
- pair_ids: int32 [8], P('dp'), may hold values from 0 to 7
- attn_weights: float32 [8, 1024, 1024], P(None, 'dp', 'tensor')
- attn_moment: float32 [8, 1024, 1024], P(None, 'dp', 'tensor')
- ffn_weights: float32 [2, 1024, 4096], P(None, 'dp', 'tensor')
- ffn_moment: float32 [2, 1024, 4096], P(None, 'dp', 'tensor')
- vectors: float32 [9, 1024], replicated
- vectors_first: float32 [9, 1024], replicated, may hold values from -56 to 56
- vectors_second: float32 [9, 1024], replicated, may hold values from 4.096 to 32.768
- head_biases: float32 [4, 1024], replicated, may hold values from -1.25 to 1.25
- head_first: float32 [4, 1024], replicated, may hold values from -16 to 16
- head_second: float32 [4, 1024], replicated, may hold values from 0.4096 to 3.2768
- ffn_bias: float32 [4096], replicated, may hold values from -1.25 to 1.25
- ffn_first: float32 [4096], replicated, may hold values from -16 to 16
- ffn_second: float32 [4096], replicated, may hold values from 0.4096 to 3.2768
Outputs:
- output: bfloat16 [8192, 1024], P(('dp', 'tensor'))
- tokens_grad: bfloat16 [8192, 1024], P(('dp', 'tensor'))
- memory_grad: bfloat16 [8192, 1024], P(('dp', 'tensor'))
- attn_moment_new: float32 [8, 1024, 1024], P(None, 'dp', 'tensor')
- attn_new: float32 [8, 1024, 1024], P(None, 'dp', 'tensor')
- ffn_moment_new: float32 [2, 1024, 4096], P(None, 'dp', 'tensor')
- ffn_new: float32 [2, 1024, 4096], P(None, 'dp', 'tensor')
- muon_rms: float32 [10], replicated
- vectors_first_new: float32 [9, 1024], replicated
- vectors_second_new: float32 [9, 1024], replicated
- vectors_new: float32 [9, 1024], replicated
- head_first_new: float32 [4, 1024], replicated
- head_second_new: float32 [4, 1024], replicated
- head_new: float32 [4, 1024], replicated
- ffn_first_new: float32 [4096], replicated
- ffn_second_new: float32 [4096], replicated
- ffn_bias_new: float32 [4096], replicated
The draws below stay inside these ranges and needn't reach their ends.
Inputs may be any that keep to these rules, and one draw needn't show every extreme that they name: In each row offsets start at 0 and rise strictly; sentence s holds memory positions offsets[r, s] up to the next offset, or 1024, minus one.
All inputs are finite; a program needn't handle non-finite values.
Results may differ from the reference program's by a relative error of at most 0.025.
Values may be sent and summed in bfloat16 or wider, within the bound.
No kernel may reach another device: no remote copies, remote signals or barrier semaphores. Data moves between devices by JAX's collectives and lax.ppermute only.
A program may use at most 128 MiB of HBM per device.

```python
import math
import jax
import jax.numpy as jnp
import numpy as np
from jax import lax

D = 1024
HEADS = 16
HEAD_DIM = 64
FF = 4096
LEN = 1024
MEM = 1024
SEGS = 4
PAIRS = 8
NS_STEPS = 5
STEP = 10
ROWS = 8
TOKENS = 8192


def draw_offsets(key, part):
    key = jax.random.fold_in(key, 11)
    row_keys = jax.random.split(key, ROWS)

    def single_row(row_key):
        cuts = jax.random.permutation(row_key, MEM - 1)[:SEGS - 1] + 1
        cuts = jnp.sort(cuts.astype(jnp.int32))
        return jnp.concatenate([jnp.zeros((1,), jnp.int32), cuts])
    return jax.vmap(single_row)(row_keys)


def draw_attn_weights(key, part):
    key = jax.random.fold_in(key, 21)
    factors = jnp.array([1.0, 1.0, 1.0, 4.0, 1.0, 1.0, 1.0, 4.0], jnp.float32) / math.sqrt(D)
    raw = jax.random.normal(key, (8, D, D), jnp.float32)
    return raw * factors[:, None, None]


def draw_ffn_weights(key, part):
    key = jax.random.fold_in(key, 22)
    factors = jnp.array([1.0 / math.sqrt(D), 1.0 / math.sqrt(FF)], jnp.float32)
    raw = jax.random.normal(key, (2, D, FF), jnp.float32)
    return raw * factors[:, None, None]


def ramped_moment(key, count, width):
    raw = jax.random.normal(key, (count, D, width), jnp.float32)
    row_ramp = 1.0 + jnp.arange(D, dtype=jnp.float32) / (D - 1)
    col_ramp = 1.0 + jnp.arange(width, dtype=jnp.float32) / (width - 1)
    return raw * (0.3 * math.sqrt(TOKENS)) * row_ramp[None, :, None] * col_ramp[None, None, :]


def draw_attn_moment(key, part):
    key = jax.random.fold_in(key, 41)
    return ramped_moment(key, 8, D)


def draw_ffn_moment(key, part):
    key = jax.random.fold_in(key, 42)
    return ramped_moment(key, 2, FF)


def draw_vectors(key, part):
    key = jax.random.fold_in(key, 31)
    raw = jax.random.normal(key, (9, D), jnp.float32)
    places = jnp.arange(9)
    is_gain = (places % 2 == 0) & (places < 6)
    return jnp.where(is_gain[:, None], 1.0 + 0.1 * raw, 0.2 * raw)


def touch_ends(values, stream_key, least, high):
    longest = values.shape.index(max(values.shape))
    spots = []
    for shift in (0, 1):
        where = [jax.random.randint(jax.random.fold_in(stream_key, axis), (), 0, length) for axis, length in enumerate(values.shape)]
        where[longest] = (where[longest] + shift) % values.shape[longest]
        spots.append(tuple(where))
    return values.at[spots[0]].set(least).at[spots[1]].set(high)


def shard_levels(own_key, dims, shards, low, largest):
    def one(axis_at, blocks):
        heights = jax.random.uniform(jax.random.fold_in(jax.random.fold_in(own_key, 6), axis_at), (blocks,), jnp.float32, low / len(shards), largest / len(shards))
        return jnp.repeat(jnp.exp(heights), dims[axis_at] // blocks).reshape((-1,) + (1,) * (len(dims) - axis_at - 1))

    level = one(*shards[0])
    for cut in shards[1:]:
        level = level * one(*cut)
    return level


def rank_table(count, slope):
    portions = [(1 << 20) // math.isqrt(standing ** slope) + 1 for standing in range(1, count + 1)]
    spread = 1 + sum(portions) // (1 << 30)
    return np.cumsum(np.array([max(1, weight // spread) for weight in portions]))


def ranked_ids(rng, extent, number_of, slope):
    table = rank_table(number_of, slope)
    ticket = jax.random.randint(jax.random.fold_in(rng, 1), extent, 0, int(table[number_of - 1]))
    rank = jnp.searchsorted(jnp.asarray(table, jnp.int32), ticket, side="right")
    return jax.random.permutation(jax.random.fold_in(rng, 2), number_of)[rank].astype(jnp.int32)


def profile(count, total, limit, lean):
    weights = [(1 << 20) // math.isqrt(grade ** lean) + 1 for grade in range(2, count + 1)]
    spare, given = total - limit - (count - 1), [1] * (count - 1)
    while spare > 0:
        movable = [i for i in range(count - 1) if given[i] < limit]
        mass, left = sum([weights[i] for i in movable]), spare
        for i in movable:
            extra = min(limit - given[i], max(1, left * weights[i] // mass), spare)
            given[i] = given[i] + extra
            spare = spare - extra
    return np.array([limit] + given)


def ragged(own_key, amount, total, most, lean):
    if amount == 2:
        one = jax.random.randint(own_key, (), max(1, total - most), min(most, total - 1) + 1)
        return jnp.stack([one, total - one])
    sizes = jnp.asarray(profile(amount, total, most, lean), jnp.int32)
    twos = (amount - 1) // 2
    source_of, sink = sizes[1:1 + 2 * twos:2], sizes[2:2 + 2 * twos:2]
    slack = jnp.minimum(source_of - 1, most - sink)
    shifted = jax.random.randint(jax.random.fold_in(own_key, 1), (twos,), 0, 1 << 20) % (slack + 1)
    sizes = sizes.at[1:1 + 2 * twos:2].set(source_of - shifted).at[2:2 + 2 * twos:2].set(sink + shifted)
    return sizes[jax.random.permutation(jax.random.fold_in(own_key, 2), amount)]


def gaussian(key, shape, spread, limit, cuts=(), held_as=jnp.bfloat16):
    values = spread * jax.random.normal(key, shape, jnp.float32)
    if cuts:
        values = values * shard_levels(key, shape, cuts, -0.22, 0.18)
    return jnp.clip(values, -limit, limit).astype(held_as)


def setup_inputs(seed: int = 0) -> dict:
    key_list = jax.random.split(jax.random.key(seed), 20)
    return {
        "tokens": gaussian(key_list[0], (TOKENS, D), 1.0, 6.0, ((0, 32),)),
        "memory": gaussian(key_list[1], (ROWS * MEM, D), 1.0, 6.0, ((0, 32),)),
        "cotangent": gaussian(key_list[2], (TOKENS, D), 1.0, 6.0, ((0, 32),)),
        "segments": jax.vmap(lambda own: jnp.searchsorted(jnp.cumsum(ragged(own, SEGS, LEN, LEN // 2, 2)), jnp.arange(LEN), side="right"))(jax.random.split(key_list[3], ROWS)).reshape((ROWS, LEN)).astype(jnp.int32),
        "offsets": draw_offsets(jax.random.fold_in(key_list[19], 71), 0),
        "pair_ids": touch_ends(ranked_ids(key_list[5], (ROWS,), PAIRS, 2), jax.random.fold_in(key_list[5], 3), 0, PAIRS - 1).astype(jnp.int32),
        "attn_weights": draw_attn_weights(jax.random.fold_in(key_list[19], 71), 0),
        "attn_moment": draw_attn_moment(jax.random.fold_in(key_list[19], 71), 0),
        "ffn_weights": draw_ffn_weights(jax.random.fold_in(key_list[19], 71), 0),
        "ffn_moment": draw_ffn_moment(jax.random.fold_in(key_list[19], 71), 0),
        "vectors": draw_vectors(jax.random.fold_in(key_list[19], 71), 0),
        "vectors_first": gaussian(key_list[11], (9, D), (0.1 * TOKENS ** 0.5), 56.0, (), jnp.float32),
        "vectors_second": jnp.clip(jnp.exp(jax.random.uniform(key_list[12], (9, D), jnp.float32, math.log(4.096), math.log(32.768))), 4.096, 32.768),
        "head_biases": gaussian(key_list[13], (4, D), 0.2, 1.25, (), jnp.float32),
        "head_first": gaussian(key_list[14], (4, D), (0.03 * TOKENS ** 0.5), 16.0, (), jnp.float32),
        "head_second": jnp.clip(jnp.exp(jax.random.uniform(key_list[15], (4, D), jnp.float32, math.log(0.4096), math.log(3.2768))), 0.4096, 3.2768),
        "ffn_bias": gaussian(key_list[16], (FF,), 0.2, 1.25, (), jnp.float32),
        "ffn_first": gaussian(key_list[17], (FF,), (0.03 * TOKENS ** 0.5), 16.0, (), jnp.float32),
        "ffn_second": jnp.clip(jnp.exp(jax.random.uniform(key_list[18], (FF,), jnp.float32, math.log(0.4096), math.log(3.2768))), 0.4096, 3.2768),
    }


@jax.custom_vjp
def low(v):
    return lax.optimization_barrier(v.astype(jnp.bfloat16)).astype(jnp.float32)

@jax.custom_vjp
def low_back(v):
    return v

def low_keep(v):
    return (low(v), None)

def low_pass(kept, grad):
    return (grad,)

def back_keep(v):
    return (v, None)

def back_low(kept, grad):
    return (low(grad),)
low.defvjp(low_keep, low_pass)
low_back.defvjp(back_keep, back_low)
EPS_NORM = 1e-05
NS_A = 3.4445
NS_B = -4.775
NS_C = 2.0315
MOMENTUM = 0.95
MUON_RATE = 0.8
MUON_DECAY = 0.01
ADAM_RATE = 0.35
BIAS_RATE = 0.25
BETA_ONE = 0.9
BETA_TWO = 0.999
ADAM_EPS = 1e-08
NEG_FILL = -1e+30
HIGH = lax.Precision.HIGHEST

def layer_norm(values, gain, shift):
    mean = lax.optimization_barrier(jnp.mean(values, axis=-1, keepdims=True))
    centered = values - mean
    variance = lax.optimization_barrier(jnp.mean(centered * centered, axis=-1, keepdims=True))
    return centered * lax.rsqrt(variance + EPS_NORM) * gain + shift

def matmul(left, right):
    return jnp.dot(left, right, precision=HIGH)

def attention_rows(query, key, value, query_seg, key_seg, causal):
    count = query_seg.shape[0]
    query_rows = query.reshape(count, -1, HEADS, HEAD_DIM)
    key_rows = key.reshape(count, -1, HEADS, HEAD_DIM)
    value_rows = value.reshape(count, -1, HEADS, HEAD_DIM)

    def single_row(pieces):
        query_row, key_row, value_row, seg_row, key_seg_row = pieces
        allowed = seg_row[:, None] == key_seg_row[None, :]
        if causal:
            places = jnp.arange(seg_row.shape[0])
            allowed = allowed & (places[:, None] >= jnp.arange(key_seg_row.shape[0])[None, :])
        scores = low_back(jnp.einsum('qhe,khe->hqk', query_row, key_row, precision=HIGH))
        scores = jnp.where(allowed[None], scores, NEG_FILL)
        peak = lax.optimization_barrier(jnp.max(scores, axis=-1, keepdims=True))
        expo = jnp.exp(scores - peak)
        probs = low(expo / lax.optimization_barrier(jnp.sum(expo, axis=-1, keepdims=True)))
        return jnp.einsum('hqk,khe->qhe', probs, value_row, precision=HIGH)
    context = lax.map(jax.checkpoint(single_row), (query_rows, key_rows, value_rows, query_seg, key_seg))
    return context.reshape(-1, HEADS * HEAD_DIM)

def orthogonal(matrix):
    squares = lax.optimization_barrier(jnp.sum(matrix * matrix, axis=(1, 2)))
    norm = jnp.sqrt(squares)[:, None, None]
    state = low(matrix / (norm + 1e-07))
    for step in range(NS_STEPS):
        gram = low(jnp.einsum('bij,bkj->bik', state, state, precision=HIGH))
        first = low(jnp.einsum('bij,bjk->bik', gram, state, precision=HIGH))
        second = jnp.einsum('bij,bjk->bik', gram, first, precision=HIGH)
        state = low(NS_A * state + NS_B * first + NS_C * second)
    rms = jnp.sqrt(squares / (matrix.shape[1] * matrix.shape[2]))
    return (state, rms)

def adam(param, first, second, grad, rate):
    first_new = BETA_ONE * first + (1.0 - BETA_ONE) * grad
    second_new = BETA_TWO * second + (1.0 - BETA_TWO) * grad * grad
    fix_one = 1.0 - BETA_ONE ** STEP
    fix_two = 1.0 - BETA_TWO ** STEP
    param_new = param - rate * (first_new / fix_one) / (jnp.sqrt(second_new / fix_two) + ADAM_EPS)
    return (first_new, second_new, param_new)

def reference(tokens, memory, cotangent, segments, offsets, pair_ids, attn_weights, attn_moment, ffn_weights, ffn_moment, vectors, vectors_first, vectors_second, head_biases, head_first, head_second, ffn_bias, ffn_first, ffn_second):
    scale = HEAD_DIM ** (-0.5)
    positions = jnp.arange(MEM)
    memory_seg = lax.optimization_barrier(jnp.sum((offsets[:, None, :] <= positions[None, :, None]).astype(jnp.int32), axis=2)) - 1

    def forward(x_in, memory_in, attn_master, ffn_master, vector_set, head_set, ffn_shift):
        attn = low(attn_master)
        ffn = low(ffn_master)
        normed_one = low(layer_norm(x_in, vector_set[0], vector_set[1]))
        query = low_back(low((matmul(normed_one, attn[0]) + head_set[0]) * scale))
        key = low_back(low(matmul(normed_one, attn[1])))
        value = low_back(low(matmul(normed_one, attn[2]) + head_set[1]))
        context = low_back(low(attention_rows(query, key, value, segments, segments, True)))
        branch = low_back(matmul(context, attn[3].T))
        after_self = x_in + branch + vector_set[6]
        normed_two = low(layer_norm(after_self, vector_set[2], vector_set[3]))
        query = low_back(low((matmul(normed_two, attn[4]) + head_set[2]) * scale))
        key = low_back(low(matmul(memory_in, attn[5])))
        value = low_back(low(matmul(memory_in, attn[6]) + head_set[3]))
        context = low_back(low(attention_rows(query, key, value, segments, memory_seg, False)))
        branch = low_back(matmul(context, attn[7].T))
        after_cross = after_self + branch + vector_set[7]
        normed_three = low(layer_norm(after_cross, vector_set[4], vector_set[5]))
        pre_hidden = low_back(matmul(normed_three, ffn[0]) + ffn_shift)
        hidden = low_back(low(jax.nn.gelu(pre_hidden, approximate=True)))
        branch = low_back(matmul(hidden, ffn[1].T))
        return after_cross + branch + vector_set[8]
    x_in = tokens.astype(jnp.float32)
    memory_in = memory.astype(jnp.float32)
    result, pullback = jax.vjp(forward, x_in, memory_in, attn_weights, ffn_weights, vectors, head_biases, ffn_bias)
    kinds = jnp.arange(PAIRS)
    onehot = (pair_ids[:, None] == kinds[None, :]).astype(jnp.float32)
    counts = lax.optimization_barrier(jnp.sum(onehot, axis=0))
    row_weight = jnp.sqrt(ROWS / (PAIRS * lax.optimization_barrier(jnp.sum(onehot * counts[None, :], axis=1))))
    token_weight = jnp.repeat(row_weight, LEN)
    grads = pullback(cotangent.astype(jnp.float32) * token_weight[:, None])
    grad_x, grad_memory, attn_grad, ffn_grad, vector_grad, head_grad, ffn_bias_grad = grads
    attn_moment_new = MOMENTUM * attn_moment + attn_grad
    ffn_moment_new = MOMENTUM * ffn_moment + ffn_grad
    attn_orth, attn_rms = orthogonal(low(attn_moment_new))
    ffn_orth, ffn_rms = orthogonal(low(ffn_moment_new))
    attn_new = attn_weights * (1.0 - MUON_RATE * MUON_DECAY) - MUON_RATE * attn_orth
    ffn_new = ffn_weights * (1.0 - MUON_RATE * MUON_DECAY) - MUON_RATE * ffn_orth
    muon_rms = jnp.concatenate([attn_rms, ffn_rms])
    vec_first, vec_second, vec_new = adam(vectors, vectors_first, vectors_second, vector_grad, ADAM_RATE)
    head_first_new, head_second_new, head_new = adam(head_biases, head_first, head_second, head_grad, BIAS_RATE)
    ffn_first_new, ffn_second_new, ffn_bias_new = adam(ffn_bias, ffn_first, ffn_second, ffn_bias_grad, BIAS_RATE)
    return (result.astype(jnp.bfloat16), grad_x.astype(jnp.bfloat16), grad_memory.astype(jnp.bfloat16), attn_moment_new, attn_new, ffn_moment_new, ffn_new, muon_rms, vec_first, vec_second, vec_new, head_first_new, head_second_new, head_new, ffn_first_new, ffn_second_new, ffn_bias_new)
```

```python
import jax
import jax.numpy as jnp
from jax import lax
from jax.sharding import PartitionSpec as P

D = 1024
HEAD_DIM = 64
FF = 4096
PAIRS = 8
NS_STEPS = 5
STEP = 10


EPS_NORM = 1e-05
NS_A = 3.4445
NS_B = -4.775
NS_C = 2.0315
MOMENTUM = 0.95
MUON_RATE = 0.8
MUON_DECAY = 0.01
ADAM_RATE = 0.35
BIAS_RATE = 0.25
BETA_ONE = 0.9
BETA_TWO = 0.999
ADAM_EPS = 1e-08
NEG_FILL = -1e30


def project(left, right):
    return jnp.dot(left, right, preferred_element_type=jnp.float32)


def project_back(left, right):
    return lax.dot_general(
        left, right, (((1,), (1,)), ((), ())), preferred_element_type=jnp.float32
    )


def rows_outer(left, right):
    return lax.dot_general(
        left, right, (((0,), (0,)), ((), ())), preferred_element_type=jnp.float32
    )


def gelu_fn(values):
    return jax.nn.gelu(values, approximate=True)


def gelu_back(values, gradient):
    unused, pull = jax.vjp(gelu_fn, values)
    return pull(gradient.astype(jnp.float32))[0]


def norm_forward(values, gain, shift):
    mean = jnp.mean(values, axis=-1, keepdims=True)
    centered = values - mean
    variance = jnp.mean(centered * centered, axis=-1, keepdims=True)
    inverse = lax.rsqrt(variance + EPS_NORM)
    plain = centered * inverse
    return (plain * gain + shift, plain, inverse)


def norm_back(grad_normed, plain, inverse, gain):
    scaled = grad_normed * gain
    mean_scaled = jnp.mean(scaled, axis=-1, keepdims=True)
    mean_cross = jnp.mean(scaled * plain, axis=-1, keepdims=True)
    grad_in = inverse * (scaled - mean_scaled - plain * mean_cross)
    return (grad_in, jnp.sum(grad_normed * plain, axis=0), jnp.sum(grad_normed, axis=0))


def allowed_mask(query_seg, key_seg, start, causal):
    allowed = query_seg[:, None] == key_seg[None, :]
    if causal:
        spots = start + jnp.arange(query_seg.shape[0])
        allowed = allowed & (spots[:, None] >= jnp.arange(key_seg.shape[0])[None, :])
    return allowed


def attend_row(query, key, value, query_seg, key_seg, causal, block):
    count = query.shape[0] // block

    def single_block(number):
        start = number * block
        part = lax.dynamic_slice_in_dim(query, start, block, 0)
        part_seg = lax.dynamic_slice_in_dim(query_seg, start, block, 0)
        scores = jnp.einsum("qhe,khe->hqk", part, key, preferred_element_type=jnp.float32)
        scores = jnp.where(allowed_mask(part_seg, key_seg, start, causal)[None], scores, NEG_FILL)
        peak = jnp.max(scores, axis=-1, keepdims=True)
        expo = jnp.exp(scores - peak)
        total = jnp.sum(expo, axis=-1, keepdims=True)
        probs = (expo / total).astype(jnp.bfloat16)
        context = jnp.einsum("hqk,khe->qhe", probs, value, preferred_element_type=jnp.float32)
        return (context.astype(jnp.bfloat16), (peak + jnp.log(total))[..., 0])

    context, log_total = lax.map(single_block, jnp.arange(count))
    return (context.reshape(query.shape), log_total)


def attend_back(query, key, value, grad_context, log_total, query_seg, key_seg, causal, block):
    count = query.shape[0] // block

    def single_block(carry, number):
        grad_key, grad_value = carry
        start = number * block
        part = lax.dynamic_slice_in_dim(query, start, block, 0)
        part_grad = lax.dynamic_slice_in_dim(grad_context, start, block, 0)
        part_seg = lax.dynamic_slice_in_dim(query_seg, start, block, 0)
        scores = jnp.einsum("qhe,khe->hqk", part, key, preferred_element_type=jnp.float32)
        scores = jnp.where(allowed_mask(part_seg, key_seg, start, causal)[None], scores, NEG_FILL)
        probs = jnp.exp(scores - log_total[number][..., None])
        grad_probs = jnp.einsum(
            "qhe,khe->hqk", part_grad, value, preferred_element_type=jnp.float32
        )
        grad_value = grad_value + jnp.einsum(
            "hqk,qhe->khe",
            probs.astype(jnp.bfloat16),
            part_grad,
            preferred_element_type=jnp.float32,
        )
        inner = jnp.sum(probs * grad_probs, axis=-1, keepdims=True)
        grad_scores = (probs * (grad_probs - inner)).astype(jnp.bfloat16)
        grad_query = jnp.einsum(
            "hqk,khe->qhe", grad_scores, key, preferred_element_type=jnp.float32
        ).astype(jnp.bfloat16)
        grad_key = grad_key + jnp.einsum(
            "hqk,qhe->khe", grad_scores, part, preferred_element_type=jnp.float32
        )
        return ((grad_key, grad_value), grad_query)

    empty = jnp.zeros(key.shape, jnp.float32)
    (grad_key, grad_value), grad_query = lax.scan(single_block, (empty, empty), jnp.arange(count))
    return (
        grad_query.reshape(query.shape),
        grad_key.astype(jnp.bfloat16),
        grad_value.astype(jnp.bfloat16),
    )


def pair_swap(values, bit):
    return lax.ppermute(values, "tensor", [(i, i ^ bit) for i in range(lax.axis_size("tensor"))])


def gather_rows(values):
    count = lax.axis_size("tensor")
    if count != 4:
        return lax.all_gather(values, "tensor", axis=0, tiled=True)
    index = lax.axis_index("tensor")
    far = pair_swap(values, 2)
    near = pair_swap(values, 1)
    cross = pair_swap(far, 1)
    height = values.shape[0]
    whole = jnp.zeros((count * height,) + values.shape[1:], values.dtype)
    for bits, part in ((0, values), (1, near), (2, far), (3, cross)):
        whole = lax.dynamic_update_slice_in_dim(whole, part, (index ^ bits) * height, 0)
    return whole


def scatter_rows(values):
    count = lax.axis_size("tensor")
    if count != 4:
        return lax.psum_scatter(
            values.astype(jnp.bfloat16), "tensor", scatter_dimension=0, tiled=True
        ).astype(jnp.float32)
    index = lax.axis_index("tensor")
    core = index % 2
    side = index // 2
    height = values.shape[0] // 4
    parts = values.reshape(2, 2, height, values.shape[1])
    away = lax.dynamic_index_in_dim(parts, 1 - core, 1, False).astype(jnp.bfloat16)
    own = lax.dynamic_index_in_dim(parts, core, 1, False)
    pair = own + pair_swap(away, 1).astype(jnp.float32)
    far = lax.dynamic_index_in_dim(pair, 1 - side, 0, False).astype(jnp.bfloat16)
    mine = lax.dynamic_index_in_dim(pair, side, 0, False)
    return mine + pair_swap(far, 2).astype(jnp.float32)


def branch_sum(values, weight):
    return scatter_rows(project_back(values, weight))


def summed_terms(terms, count):
    total = jnp.zeros((count, terms[0][1].shape[0]), jnp.float32)
    for gradient, weight in terms:
        total = total + project_back(gradient, weight)
    return total


def input_sum(terms, local_rows):
    return scatter_rows(summed_terms(terms, lax.axis_size("tensor") * local_rows))


def squares_of(values):
    wide = values.astype(jnp.float32)
    return jnp.sum(wide * wide, axis=(1, 2))


def rms_of(attn_low_moment, ffn_low_moment):
    attn_total, ffn_total = lax.psum(
        (squares_of(attn_low_moment), squares_of(ffn_low_moment)), ("dp", "tensor")
    )
    return jnp.concatenate([jnp.sqrt(attn_total / (D * D)), jnp.sqrt(ffn_total / (D * FF))])


def gram_of(state):
    return lax.dot_general(
        state, state, (((1,), (1,)), ((), ())), preferred_element_type=jnp.float32
    )


def next_state(state, first, second):
    return (
        NS_A * state.astype(jnp.float32) + NS_B * first.astype(jnp.float32) + NS_C * second
    ).astype(jnp.bfloat16)


def attn_orthogonal(low_moment):
    count, width = low_moment.shape[0], low_moment.shape[2]
    columns = lax.all_to_all(low_moment, "dp", split_axis=0, concat_axis=1, tiled=True)[0]
    index = lax.axis_index("tensor")
    near = jnp.concatenate([columns, pair_swap(columns, 1)], axis=1)
    far = pair_swap(columns, 2)
    whole = jnp.concatenate([near, far, pair_swap(far, 1)], axis=1)
    wide = whole.astype(jnp.float32)
    state = (wide / (jnp.sqrt(jnp.sum(wide * wide)) + 1e-07)).astype(jnp.bfloat16)
    for step in range(NS_STEPS):
        gram = gram_of(state).astype(jnp.bfloat16)
        if step == NS_STEPS - 1:
            state = state[:, :width]
        first = project(gram, state).astype(jnp.bfloat16)
        second = project(gram, first)
        state = next_state(state, first, second)
    return lax.all_to_all(
        state.reshape(count, -1, width), "dp", split_axis=0, concat_axis=0, tiled=True
    )


def ffn_orthogonal(low_moment):
    rows, width = low_moment.shape[1], low_moment.shape[2]
    index = lax.axis_index("tensor")
    side = index // 2
    keep = lax.dynamic_index_in_dim(low_moment, side, 0, False)
    send = lax.dynamic_index_in_dim(low_moment, 1 - side, 0, False)
    block = jnp.concatenate([keep, pair_swap(send, 2)], axis=1)
    half = lax.all_gather(block, "dp", axis=0, tiled=True)
    wide = half.astype(jnp.float32)
    own_squares = jnp.sum(wide * wide)[None]
    squares = own_squares + pair_swap(own_squares, 1)
    state = (wide / (jnp.sqrt(squares) + 1e-07)).astype(jnp.bfloat16)
    start = lax.axis_index("dp") * rows
    for step in range(NS_STEPS):
        part = gram_of(state).astype(jnp.bfloat16)
        gram = (part.astype(jnp.float32) + pair_swap(part, 1).astype(jnp.float32)).astype(
            jnp.bfloat16
        )
        left, kept = gram, state
        if step == NS_STEPS - 1:
            left = lax.dynamic_slice_in_dim(gram, start, rows, 0)
            kept = lax.dynamic_slice_in_dim(state, start, rows, 0)
        mixed = (NS_B * left.astype(jnp.float32) + NS_C * project(left, gram)).astype(jnp.bfloat16)
        state = (NS_A * kept.astype(jnp.float32) + project(mixed, state)).astype(jnp.bfloat16)
    mine, other = state[:, :width], pair_swap(state[:, width:], 2)
    return jnp.where(side == 0, jnp.stack([mine, other]), jnp.stack([other, mine]))


def newton_schulz(attn_low_moment, ffn_low_moment):
    if lax.axis_size("tensor") == 4 and lax.axis_size("dp") == attn_low_moment.shape[0]:
        return (
            attn_orthogonal(attn_low_moment).astype(jnp.float32),
            ffn_orthogonal(ffn_low_moment).astype(jnp.float32),
            rms_of(attn_low_moment, ffn_low_moment),
        )
    attn_total, ffn_total = lax.psum(
        (squares_of(attn_low_moment), squares_of(ffn_low_moment)), ("dp", "tensor")
    )
    rms_values = jnp.concatenate([jnp.sqrt(attn_total / (D * D)), jnp.sqrt(ffn_total / (D * FF))])
    attn_state = (
        attn_low_moment.astype(jnp.float32) / (jnp.sqrt(attn_total)[:, None, None] + 1e-07)
    ).astype(jnp.bfloat16)
    ffn_state = (
        ffn_low_moment.astype(jnp.float32) / (jnp.sqrt(ffn_total)[:, None, None] + 1e-07)
    ).astype(jnp.bfloat16)
    for step in range(NS_STEPS):
        attn_full, ffn_full = (
            lax.all_gather(attn_state, "dp", axis=1, tiled=True),
            lax.all_gather(ffn_state, "dp", axis=1, tiled=True),
        )
        attn_gram = jnp.einsum(
            "mrc,mkc->mrk", attn_state, attn_full, preferred_element_type=jnp.float32
        )
        ffn_gram = jnp.einsum(
            "mrc,mkc->mrk", ffn_state, ffn_full, preferred_element_type=jnp.float32
        )
        attn_gram, ffn_gram = (
            lax.psum(attn_gram.astype(jnp.bfloat16), "tensor").astype(jnp.float32),
            lax.psum(ffn_gram.astype(jnp.bfloat16), "tensor").astype(jnp.float32),
        )
        attn_gram = attn_gram.astype(jnp.bfloat16)
        ffn_gram = ffn_gram.astype(jnp.bfloat16)
        attn_first = jnp.einsum(
            "mrk,mkc->mrc", attn_gram, attn_full, preferred_element_type=jnp.float32
        ).astype(jnp.bfloat16)
        ffn_first = jnp.einsum(
            "mrk,mkc->mrc", ffn_gram, ffn_full, preferred_element_type=jnp.float32
        ).astype(jnp.bfloat16)
        attn_first_full, ffn_first_full = (
            lax.all_gather(attn_first, "dp", axis=1, tiled=True),
            lax.all_gather(ffn_first, "dp", axis=1, tiled=True),
        )
        attn_second = jnp.einsum(
            "mrk,mkc->mrc", attn_gram, attn_first_full, preferred_element_type=jnp.float32
        )
        ffn_second = jnp.einsum(
            "mrk,mkc->mrc", ffn_gram, ffn_first_full, preferred_element_type=jnp.float32
        )
        attn_state = (
            NS_A * attn_state.astype(jnp.float32)
            + NS_B * attn_first.astype(jnp.float32)
            + NS_C * attn_second
        ).astype(jnp.bfloat16)
        ffn_state = (
            NS_A * ffn_state.astype(jnp.float32)
            + NS_B * ffn_first.astype(jnp.float32)
            + NS_C * ffn_second
        ).astype(jnp.bfloat16)
    return (attn_state.astype(jnp.float32), ffn_state.astype(jnp.float32), rms_values)


def adam(param, first, second, gradient, rate):
    first_new = BETA_ONE * first + (1.0 - BETA_ONE) * gradient
    second_new = BETA_TWO * second + (1.0 - BETA_TWO) * gradient * gradient
    fix_one = 1.0 - BETA_ONE**STEP
    fix_two = 1.0 - BETA_TWO**STEP
    param_new = param - rate * (first_new / fix_one) / (jnp.sqrt(second_new / fix_two) + ADAM_EPS)
    return (first_new, second_new, param_new)


def local(
    tokens,
    memory,
    cotangent,
    segments,
    offsets,
    pair_ids,
    attn_weights,
    attn_moment,
    ffn_weights,
    ffn_moment,
    vectors,
    vectors_first,
    vectors_second,
    head_biases,
    head_first,
    head_second,
    ffn_bias,
    ffn_first,
    ffn_second,
):
    rows = segments.shape[0]
    length = segments.shape[1]
    local_rows = tokens.shape[0]
    memory_rows = memory.shape[0]
    tensor_count = lax.axis_size("tensor")
    source_length = memory_rows * tensor_count // rows
    head_width = attn_weights.shape[2]
    hidden_width = ffn_weights.shape[2]
    heads_here = head_width // HEAD_DIM
    block = min(512, length)
    scale = HEAD_DIM ** (-0.5)
    tensor_index = lax.axis_index("tensor")

    def split_heads(values, steps):
        return values.reshape(rows, steps, heads_here, HEAD_DIM)

    positions = jnp.arange(source_length)
    memory_seg = (
        jnp.sum((offsets[:, None, :] <= positions[None, :, None]).astype(jnp.int32), axis=2) - 1
    )
    head_own = lax.dynamic_slice_in_dim(head_biases, tensor_index * head_width, head_width, 1)
    kinds = jnp.arange(PAIRS)
    onehot = (pair_ids[:, None] == kinds[None, :]).astype(jnp.float32)
    counts = lax.psum(jnp.sum(onehot, axis=0), "dp")
    all_rows = rows * lax.axis_size("dp")
    row_weight = jnp.sqrt(all_rows / (PAIRS * jnp.sum(onehot * counts[None, :], axis=1)))
    attn_low, ffn_low = (
        lax.all_gather(attn_weights.astype(jnp.bfloat16), "dp", axis=1, tiled=True),
        lax.all_gather(ffn_weights.astype(jnp.bfloat16), "dp", axis=1, tiled=True),
    )
    x_in = tokens.astype(jnp.float32)
    normed_one, plain_one, inverse_one = norm_forward(x_in, vectors[0], vectors[1])
    gathered_one, memory_all = (
        gather_rows(normed_one.astype(jnp.bfloat16)),
        gather_rows(memory),
    )
    query_self = ((project(gathered_one, attn_low[0]) + head_own[0]) * scale).astype(jnp.bfloat16)
    key_self = project(gathered_one, attn_low[1]).astype(jnp.bfloat16)
    value_self = (project(gathered_one, attn_low[2]) + head_own[1]).astype(jnp.bfloat16)

    def self_row(pieces):
        return attend_row(pieces[0], pieces[1], pieces[2], pieces[3], pieces[3], True, block)

    context_self, logsum_self = lax.map(
        self_row,
        (
            split_heads(query_self, length),
            split_heads(key_self, length),
            split_heads(value_self, length),
            segments,
        ),
    )
    context_self = context_self.reshape(rows * length, head_width)
    after_self = x_in + branch_sum(context_self, attn_low[3]) + vectors[6]
    normed_two, plain_two, inverse_two = norm_forward(after_self, vectors[2], vectors[3])
    gathered_two = gather_rows(normed_two.astype(jnp.bfloat16))
    query_cross = ((project(gathered_two, attn_low[4]) + head_own[2]) * scale).astype(jnp.bfloat16)
    key_cross = project(memory_all, attn_low[5]).astype(jnp.bfloat16)
    value_cross = (project(memory_all, attn_low[6]) + head_own[3]).astype(jnp.bfloat16)

    def cross_row(pieces):
        return attend_row(pieces[0], pieces[1], pieces[2], pieces[3], pieces[4], False, block)

    context_cross, logsum_cross = lax.map(
        cross_row,
        (
            split_heads(query_cross, length),
            split_heads(key_cross, source_length),
            split_heads(value_cross, source_length),
            segments,
            memory_seg,
        ),
    )
    context_cross = context_cross.reshape(rows * length, head_width)
    after_cross = after_self + branch_sum(context_cross, attn_low[7]) + vectors[7]
    normed_three, plain_three, inverse_three = norm_forward(after_cross, vectors[4], vectors[5])
    low_three = normed_three.astype(jnp.bfloat16)
    inputs_three = gather_rows(low_three)
    bias_own = lax.dynamic_slice_in_dim(ffn_bias, tensor_index * hidden_width, hidden_width, 0)
    pre_hidden = project(inputs_three, ffn_low[0]) + bias_own
    hidden = gelu_fn(pre_hidden).astype(jnp.bfloat16)
    ffn_out = branch_sum(hidden, ffn_low[1])
    result = after_cross + ffn_out + vectors[8]
    places = tensor_index * local_rows + jnp.arange(local_rows)
    member = (places[:, None] // length == jnp.arange(rows)[None, :]).astype(jnp.float32)
    token_weight = jnp.sum(member * row_weight[None, :], axis=1)
    grad_out = cotangent.astype(jnp.float32) * token_weight[:, None]
    grad_low = gather_rows(grad_out.astype(jnp.bfloat16))
    grad_hidden = project(grad_low, ffn_low[1]).astype(jnp.bfloat16)
    grad_down = rows_outer(grad_low, hidden)
    grad_pre = gelu_back(pre_hidden, grad_hidden).astype(jnp.bfloat16)
    grad_up = rows_outer(inputs_three, grad_pre)
    ffn_part = jnp.stack([grad_up, grad_down])
    bias_grad_full = lax.dynamic_update_slice_in_dim(
        jnp.zeros((hidden_width * tensor_count,), jnp.float32),
        jnp.sum(grad_pre.astype(jnp.float32), axis=0),
        tensor_index * hidden_width,
        0,
    )
    grad_three = input_sum(((grad_pre, ffn_low[0]),), local_rows)
    back_three, gain_three, shift_three = norm_back(
        grad_three, plain_three, inverse_three, vectors[4]
    )
    grad_cross = grad_out + back_three
    grad_branch_cross = gather_rows(grad_cross.astype(jnp.bfloat16))
    grad_context_cross = project(grad_branch_cross, attn_low[7]).astype(jnp.bfloat16)
    grad_out_cross = rows_outer(grad_branch_cross, context_cross)

    def cross_back(pieces):
        return attend_back(
            pieces[0],
            pieces[1],
            pieces[2],
            pieces[3],
            pieces[4],
            pieces[5],
            pieces[6],
            False,
            block,
        )

    grad_query_cross, grad_key_cross, grad_value_cross = lax.map(
        cross_back,
        (
            split_heads(query_cross, length),
            split_heads(key_cross, source_length),
            split_heads(value_cross, source_length),
            split_heads(grad_context_cross, length),
            logsum_cross,
            segments,
            memory_seg,
        ),
    )
    grad_query_cross = (
        grad_query_cross.reshape(rows * length, head_width).astype(jnp.float32) * scale
    ).astype(jnp.bfloat16)
    grad_key_cross = grad_key_cross.reshape(rows * source_length, head_width)
    grad_value_cross = grad_value_cross.reshape(rows * source_length, head_width)
    grad_query_weight_cross = rows_outer(gathered_two, grad_query_cross)
    grad_key_weight_cross = rows_outer(memory_all, grad_key_cross)
    grad_value_weight_cross = rows_outer(memory_all, grad_value_cross)
    memory_grad = input_sum(
        ((grad_key_cross, attn_low[5]), (grad_value_cross, attn_low[6])), memory_rows
    ).astype(jnp.bfloat16)
    grad_two = input_sum(((grad_query_cross, attn_low[4]),), local_rows)
    back_two, gain_two, shift_two = norm_back(grad_two, plain_two, inverse_two, vectors[2])
    grad_self = grad_cross + back_two
    grad_branch_self = gather_rows(grad_self.astype(jnp.bfloat16))
    grad_context_self = project(grad_branch_self, attn_low[3]).astype(jnp.bfloat16)
    grad_out_self = rows_outer(grad_branch_self, context_self)

    def self_back(pieces):
        return attend_back(
            pieces[0], pieces[1], pieces[2], pieces[3], pieces[4], pieces[5], pieces[5], True, block
        )

    grad_query_self, grad_key_self, grad_value_self = lax.map(
        self_back,
        (
            split_heads(query_self, length),
            split_heads(key_self, length),
            split_heads(value_self, length),
            split_heads(grad_context_self, length),
            logsum_self,
            segments,
        ),
    )
    grad_query_self = (
        grad_query_self.reshape(rows * length, head_width).astype(jnp.float32) * scale
    ).astype(jnp.bfloat16)
    grad_key_self = grad_key_self.reshape(rows * length, head_width)
    grad_value_self = grad_value_self.reshape(rows * length, head_width)
    grad_query_weight_self = rows_outer(gathered_one, grad_query_self)
    grad_key_weight_self = rows_outer(gathered_one, grad_key_self)
    grad_value_weight_self = rows_outer(gathered_one, grad_value_self)
    grad_one = input_sum(
        (
            (grad_query_self, attn_low[0]),
            (grad_key_self, attn_low[1]),
            (grad_value_self, attn_low[2]),
        ),
        local_rows,
    )
    back_one, gain_one, shift_one = norm_back(grad_one, plain_one, inverse_one, vectors[0])
    tokens_grad = (grad_self + back_one).astype(jnp.bfloat16)
    vector_grad = jnp.stack(
        [
            gain_one,
            shift_one,
            gain_two,
            shift_two,
            gain_three,
            shift_three,
            jnp.sum(grad_self, axis=0),
            jnp.sum(grad_cross, axis=0),
            jnp.sum(grad_out, axis=0),
        ]
    )
    head_grad_own = jnp.stack(
        [
            jnp.sum(grad_query_self.astype(jnp.float32), axis=0),
            jnp.sum(grad_value_self.astype(jnp.float32), axis=0),
            jnp.sum(grad_query_cross.astype(jnp.float32), axis=0),
            jnp.sum(grad_value_cross.astype(jnp.float32), axis=0),
        ]
    )
    head_grad_full = lax.dynamic_update_slice_in_dim(
        jnp.zeros((4, head_width * tensor_count), jnp.float32),
        head_grad_own,
        tensor_index * head_width,
        1,
    )
    vector_total, head_total, bias_total = lax.psum(
        (vector_grad, head_grad_full, bias_grad_full), ("dp", "tensor")
    )
    attn_grad = jnp.stack(
        [
            grad_query_weight_self,
            grad_key_weight_self,
            grad_value_weight_self,
            grad_out_self,
            grad_query_weight_cross,
            grad_key_weight_cross,
            grad_value_weight_cross,
            grad_out_cross,
        ]
    )
    attn_part, ffn_rows = (
        lax.psum_scatter(
            attn_grad.astype(jnp.bfloat16), "dp", scatter_dimension=1, tiled=True
        ).astype(jnp.float32),
        lax.psum_scatter(
            ffn_part.astype(jnp.bfloat16), "dp", scatter_dimension=1, tiled=True
        ).astype(jnp.float32),
    )
    attn_moment_new = MOMENTUM * attn_moment + attn_part
    ffn_moment_new = MOMENTUM * ffn_moment + ffn_rows
    attn_step, ffn_step, muon_rms = newton_schulz(
        attn_moment_new.astype(jnp.bfloat16), ffn_moment_new.astype(jnp.bfloat16)
    )
    attn_new = attn_weights * (1.0 - MUON_RATE * MUON_DECAY) - MUON_RATE * attn_step
    ffn_new = ffn_weights * (1.0 - MUON_RATE * MUON_DECAY) - MUON_RATE * ffn_step
    vec_first, vec_second, vec_new = adam(
        vectors, vectors_first, vectors_second, vector_total, ADAM_RATE
    )
    head_first_new, head_second_new, head_new = adam(
        head_biases, head_first, head_second, head_total, BIAS_RATE
    )
    ffn_first_new, ffn_second_new, ffn_bias_new = adam(
        ffn_bias, ffn_first, ffn_second, bias_total, BIAS_RATE
    )
    return (
        result.astype(jnp.bfloat16),
        tokens_grad,
        memory_grad,
        attn_moment_new,
        attn_new,
        ffn_moment_new,
        ffn_new,
        muon_rms,
        vec_first,
        vec_second,
        vec_new,
        head_first_new,
        head_second_new,
        head_new,
        ffn_first_new,
        ffn_second_new,
        ffn_bias_new,
    )


def solution(mesh):
    placed = (
        P(("dp", "tensor"), None),
        P(("dp", "tensor"), None),
        P(("dp", "tensor"), None),
        P("dp", None),
        P("dp", None),
        P("dp"),
        P(None, "dp", "tensor"),
        P(None, "dp", "tensor"),
        P(None, "dp", "tensor"),
        P(None, "dp", "tensor"),
        P(),
        P(),
        P(),
        P(),
        P(),
        P(),
        P(),
        P(),
        P(),
    )
    return jax.shard_map(
        local,
        mesh=mesh,
        in_specs=placed,
        out_specs=(
            P(("dp", "tensor"), None),
            P(("dp", "tensor"), None),
            P(("dp", "tensor"), None),
            P(None, "dp", "tensor"),
            P(None, "dp", "tensor"),
            P(None, "dp", "tensor"),
            P(None, "dp", "tensor"),
            P(),
            P(),
            P(),
            P(),
            P(),
            P(),
            P(),
            P(),
            P(),
            P(),
        ),
        check_vma=False,
    )
```
